256 devices in a mesh: term: 8 (over y, core), sector: 32 (over z, x).
Axes of the slice: x: 4, y: 4, z: 8, core: 2. Of those that a mesh axis runs over, the one named last changes fastest.
Arguments:
- wavefunction: bfloat16 [32, 3, 256, 256], P('sector'), may hold values from -6 to 6
- left_operators: bfloat16 [32, 256, 256, 256], P('sector', 'term'), may hold values from -0.0234375 to 0.0234375
- right_operators: bfloat16 [32, 256, 256, 256], P('sector', 'term'), may hold values from -0.375 to 0.375
- target_sector: int32 [32, 256, 1], P('sector', 'term'), may hold values from 0 to 31; in each aligned block of 32 rows (0 to 31, 32 to 63, ..., all dimensions but the last counted through in order) at most 2 rows name the same one
Outputs:
- sigma_blocks: float32 [32, 3, 256, 256], P('sector', None, 'term')
The draws below stay inside these ranges and needn't reach their ends.
Inputs may be any that keep to these rules, and one draw needn't show every extreme that they name: `target_sector`: in each aligned block of 32 terms of one source sector no target appears more than 2 times, and some block reaches 2.
All inputs are finite; a program needn't handle non-finite values.
Results may differ from the reference program's by a relative error of at most 0.017.
Values may be sent and summed in bfloat16 or wider, within the bound.
No kernel may reach another device: no remote copies, remote signals or barrier semaphores. Data moves between devices by JAX's collectives and lax.ppermute only.
A program may use at most 128 MiB of HBM per device.

```python
import math
import jax
import jax.numpy as jnp
import numpy as np
from jax import lax

K = 256
NVEC = 3
TERM_DEV = 32
TERMS = 256
NSEC = 32
CAP = 2


def block_levels(key, dims, cuts, low, high):
    def one(dim, blocks):
        steps = jax.random.uniform(jax.random.fold_in(jax.random.fold_in(key, 6), dim), (blocks,), jnp.float32, low / len(cuts), high / len(cuts))
        return jnp.repeat(jnp.exp(steps), dims[dim] // blocks).reshape((-1,) + (1,) * (len(dims) - dim - 1))

    level = one(*cuts[0])
    for cut in cuts[1:]:
        level = level * one(*cut)
    return level


def assign_block(stream_key, own, number, rows, count, top, most, lean):
    ranking = jax.random.permutation(stream_key, count)
    crowded, usual = portions_of(count, rows * top, most, lean, True), portions_of(count, rows * top, most, lean, False)
    places = jnp.arange(count)

    def named(lengths, rotation):
        used = int((lengths > 0).sum())
        fixed = max(1, used // 4)
        passed = fixed + (places - fixed + rotation * (used - fixed)) % max(1, count - fixed)
        return jnp.zeros((count,), jnp.int32).at[ranking[jnp.where(places < fixed, places, passed)]].set(jnp.asarray(lengths, jnp.int32))

    lengths = jnp.where(number % 4 == 0, named(crowded, number // 4), named(usual, number - number // 4 - 1))
    mixed = jax.random.permutation(jax.random.fold_in(own, 3), count)
    donor, taker = mixed[0:count // 2 * 2:2], mixed[1:count // 2 * 2:2]
    slack = jnp.minimum(lengths[donor] - 1, most - lengths[taker]) // 2
    slack = jnp.where((donor == ranking[0]) | (taker == ranking[0]) | (lengths[taker] == 0), 0, jnp.maximum(slack, 0))
    passed = jax.random.randint(jax.random.fold_in(own, 4), (count // 2,), 0, 1 << 20) % (slack + 1)
    lengths = lengths.at[donor].add(-passed).at[taker].add(passed)
    items = jnp.searchsorted(jnp.cumsum(lengths), jnp.arange(rows * top), side="right").astype(jnp.int32)
    listing = items.reshape(top, rows).T
    listing = listing[jax.random.permutation(jax.random.fold_in(own, 1), rows)]
    rotation = jax.random.randint(jax.random.fold_in(own, 2), (rows, 1), 0, top)
    return jnp.take_along_axis(listing, (jnp.arange(top)[None, :] + rotation) % top, axis=1)


def portions_of(amount, total, limit, skew, full):
    loads = [(1 << 20) // math.isqrt(rank ** skew) + 1 for rank in range(1, amount + 1)]
    largest = limit if full else min(limit, max(-(-total // amount), total * loads[0] // sum(loads)))
    least = 1 if total - largest >= amount - 1 else 0
    holding, rest = [largest] + [least] * (amount - 1), total - largest - least * (amount - 1)
    while rest > 0:
        candidates = [i for i in range(1, amount) if holding[i] < largest] or [i for i in range(1, amount) if holding[i] < limit]
        whole, budget = sum([loads[i] for i in candidates]), rest
        for i in candidates:
            addition = min(limit - holding[i], max(1, budget * loads[i] // whole), rest)
            holding[i] = holding[i] + addition
            rest = rest - addition
    return np.array(holding)


def bell_draw(own_key, shape, spread, most, shards=(), kind=jnp.bfloat16):
    loudness = block_levels(own_key, shape, shards, -0.22, 0.18) if shards else 1.0
    values = jax.random.normal(own_key, shape, jnp.float32) * spread * loudness
    return jnp.minimum(jnp.maximum(values, -most), most).astype(kind)


def setup_inputs(seed: int = 0) -> dict:
    splits = jax.random.split(jax.random.key(seed), 5)
    wavefunction = bell_draw(splits[0], (NSEC, NVEC, K, K), 1.0, 6.0, ((0, 32),))
    left_operators = bell_draw(splits[1], (NSEC, TERMS, K, K), (K * TERMS) ** -0.5, 0.0234375, ((0, 32), (1, 8)))
    right_operators = bell_draw(splits[2], (NSEC, TERMS, K, K), K ** -0.5, 0.375, ((0, 32), (1, 8)))
    target_sector_keys = jax.random.split(jax.random.fold_in(splits[3], 1), NSEC * TERMS // TERM_DEV)
    target_sector_turns = jax.random.permutation(jax.random.fold_in(splits[3], 3), NSEC * TERMS // TERM_DEV)
    target_sector = jax.vmap(lambda own, number: assign_block(jax.random.fold_in(splits[3], 2), own, number, TERM_DEV, NSEC, 1, CAP, 2))(target_sector_keys, target_sector_turns).reshape((NSEC, TERMS, 1))
    return dict(wavefunction=wavefunction, left_operators=left_operators, right_operators=right_operators, target_sector=target_sector)


def reference(wavefunction, left_operators, right_operators, target_sector):
    def per_sector(sigma_sum, inputs):
        local_wavefunction, left_here, right_here, target_here = inputs
        wavefunction_single = local_wavefunction.astype(jnp.float32)

        def per_term(operands):
            single_left_operator, single_right_operator = operands
            partial_contraction = jnp.einsum("nzd,ud->nzu", wavefunction_single, single_right_operator.astype(jnp.float32)).astype(jnp.bfloat16)
            partial_contraction = lax.optimization_barrier(partial_contraction)
            sigma_product = jnp.einsum("po,dok->dpk", single_left_operator.astype(jnp.float32), partial_contraction.astype(jnp.float32))
            return sigma_product.astype(jnp.bfloat16)

        products = lax.map(per_term, (left_here, right_here))
        products = lax.optimization_barrier(products)
        group_count = products.shape[0] // TERM_DEV
        grouped = products.reshape((group_count, TERM_DEV) + products.shape[1:])
        group_targets = target_here[:, 0].astype(jnp.int32).reshape(group_count, TERM_DEV)

        def per_group(total, group_inputs):
            group_products, group_target = group_inputs
            local_sum = jnp.zeros(sigma_sum.shape, jnp.float32).at[group_target].add(group_products.astype(jnp.float32))
            rounded = lax.optimization_barrier(local_sum.astype(jnp.bfloat16))
            return total + rounded.astype(jnp.float32), None

        sigma_sum, unused_groups = lax.scan(per_group, sigma_sum, (grouped, group_targets))
        return sigma_sum, None

    start = jnp.zeros(wavefunction.shape, jnp.float32)
    sigma_sum, unused_out = lax.scan(per_sector, start, (wavefunction, left_operators, right_operators, target_sector))
    return sigma_sum
```

```python
import functools

import jax
import jax.numpy as jnp
import numpy as np
from jax import lax
from jax.experimental import pallas as pl
from jax.experimental.pallas import tpu as pltpu
from jax.sharding import Mesh, PartitionSpec as P

AXES = ("y", "c", "z", "x")
SIZES = (4, 2, 8, 4)
K = 256
TERMS = 32
ROWS = 32
PER_STEP = 4


def gray(n):
    return n ^ (n >> 1)


def ring_slot(distance, core):
    return gray(jnp.where(core == 0, (4 - distance) & 3, distance))


def ring_distance(slot, core):
    distance = gray(slot)
    return jnp.where(core == 0, (4 - distance) & 3, distance)


def ring_flip(step, core):
    return 1 if step == core else 3


def layout_z(b_z, b_x, z, x, c):
    distance = ((b_z - c) & 7) ^ ((z - c) & 7)
    slot = (distance & 1) * 4 + ring_slot(distance >> 1, c)
    return slot * 16 + b_x


def layout_x(b_z, b_x, z, x, c):
    return ring_slot(b_x ^ x, c) * 32 + b_z


def layout_y(b_z, b_x, z, x, c):
    return (b_x ^ x) * 8 + b_z


LAYOUTS = {
    "z": (layout_z, 4, lambda j, y, c: j),
    "x": (layout_x, 8, lambda j, y, c: y ^ j),
    "y": (layout_y, 32, lambda j, y, c: y ^ ring_distance(j, c)),
}


def products_kernel(first, place_ref, psi_ref, left_ref, right_ref, keep_ref, send_ref):
    layout, stride, row_owner = LAYOUTS[first]
    step = pl.program_id(0)
    y, c, z, x = (place_ref[TERMS + i] for i in range(4))

    @pl.when(step == 0)
    def _():
        keep_ref[...] = jnp.zeros_like(keep_ref)
        send_ref[...] = jnp.zeros_like(send_ref)

    cores = (c, 1 - c)
    owners = [(row_owner(j, y, core) * 2 + core) * ROWS for core in cores for j in range(4)]
    rows = [pl.multiple_of(o, ROWS) for o in owners]
    psi = psi_ref[...]
    left = jnp.concatenate([left_ref[t, pl.ds(r, ROWS), :] for t in range(PER_STEP) for r in rows], axis=0)
    turned = jnp.dot(left, psi, preferred_element_type=jnp.float32).astype(jnp.bfloat16)
    for t in range(PER_STEP):
        product = lax.dot_general(
            turned[t * K:(t + 1) * K], right_ref[t], (((1,), (1,)), ((), ())), preferred_element_type=jnp.float32
        )
        target = place_ref[step * PER_STEP + t]
        for part, ref in enumerate((keep_ref, send_ref)):
            base = layout(target >> 2, target & 3, z, x, cores[part])
            for j in range(4):
                value = product[(part * 4 + j) * ROWS:(part * 4 + j + 1) * ROWS]
                at = base + j * stride
                ref[at] = (ref[at].astype(jnp.float32) + value).astype(jnp.bfloat16)


def local_sums(first, place, psi, left, right):
    block = pl.BlockSpec((PER_STEP, K, K), lambda i, place: (i, 0, 0))
    whole = pl.BlockSpec((128, ROWS, K), lambda i, place: (0, 0, 0))
    shape = jax.ShapeDtypeStruct((128, ROWS, K), jnp.bfloat16)
    return pl.pallas_call(
        functools.partial(products_kernel, first),
        grid_spec=pltpu.PrefetchScalarGridSpec(
            num_scalar_prefetch=1,
            grid=(TERMS // PER_STEP,),
            in_specs=[pl.BlockSpec((K, K), lambda i, place: (0, 0)), block, block],
            out_specs=[whole, whole],
        ),
        out_shape=[shape, shape],
        compiler_params=pltpu.CompilerParams(vmem_limit_bytes=24 * 2**20),
        cost_estimate=pl.CostEstimate(flops=4 * TERMS * K**3, bytes_accessed=13 * 2**20, transcendentals=0),
    )(place, psi, left, right)


def permutation(move):
    pairs = []
    for index in range(256):
        place = [int(v) for v in np.unravel_index(index, SIZES)]
        pairs.append((index, int(np.ravel_multi_index(move(*place), SIZES))))
    return pairs


def core_swap(a):
    return lax.ppermute(a, AXES, permutation(lambda y, c, z, x: (y, 1 - c, z, x)))


def ring_swap(a, axis, step):
    if axis == "x":
        return lax.ppermute(a, AXES, permutation(lambda y, c, z, x: (y, c, z, x ^ ring_flip(step, c))))
    return lax.ppermute(a, AXES, permutation(lambda y, c, z, x: (y ^ ring_flip(step, c), c, z, x)))


def far_swap(a, axis, distance):
    if axis == "x":
        return lax.ppermute(a, AXES, permutation(lambda y, c, z, x: (y, c, z, x ^ distance)))
    return lax.ppermute(a, AXES, permutation(lambda y, c, z, x: (y ^ distance, c, z, x)))


def z_swap(a, step):
    def move(y, c, z, x):
        flip = 1 if step == 0 else 2 * ring_flip(step - 1, c)
        return (y, c, ((((z - c) % 8) ^ flip) + c) % 8, x)

    return lax.ppermute(a, AXES, permutation(move))


def total(*arrays):
    value = arrays[0].astype(jnp.float32)
    for a in arrays[1:]:
        value = value + a.astype(jnp.float32)
    return value


def rounded(*arrays):
    return total(*arrays).astype(jnp.bfloat16)


def halve_ring(parts, axis):
    first = ring_swap(rounded(*(a[2:] for a in parts)), axis, 0)
    second = ring_swap(rounded(*(a[1] for a in parts), first[1]), axis, 1)
    return [*(a[0] for a in parts), first[0], second]


def direct_ring(parts, axis):
    mine = rounded(*parts)
    return [mine[0]] + [far_swap(mine[d], axis, d) for d in (1, 2, 3)]


def halve_z(parts):
    first = z_swap(rounded(*(a[4:] for a in parts)), 0)
    parts = [*(a[:4] for a in parts), first]
    second = z_swap(rounded(*(a[2:] for a in parts)), 1)
    third = z_swap(rounded(*(a[1] for a in parts), second[1]), 2)
    return [*(a[0] for a in parts), second[0], third]


def body(wavefunction, left_operators, right_operators, target_sector):
    psi, left, right = wavefunction[0], left_operators[0], right_operators[0]
    here = jnp.stack([lax.axis_index(a) for a in AXES]).astype(jnp.int32)
    place = jnp.concatenate([target_sector[0, :, 0], here])
    shape = (ROWS, K)

    def part(first, vector, dims):
        keep, send = local_sums(first, place, psi[vector], left, right)
        return [keep.reshape(dims + shape), core_swap(send).reshape(dims + shape)]

    part_z = part("z", 0, (8, 4, 4))
    part_x = part("x", 1, (4, 4, 8))
    part_y = part("y", 2, (4, 4, 8))
    part_z = halve_z(part_z)
    part_x = halve_ring(part_x, "x")
    part_y = halve_ring(part_y, "y")
    part_x = direct_ring(part_x, "y")
    part_y = direct_ring(part_y, "x")
    spread = lax.all_to_all(rounded(*part_z).reshape((16,) + shape), ("y", "x"), 0, 0, tiled=True)
    out_z = jnp.sum(spread.astype(jnp.float32), axis=0)
    both = jnp.stack([rounded(*part_x), rounded(*part_y)], axis=1)
    spread = lax.all_to_all(both, "z", 0, 0, tiled=True)
    out_xy = jnp.sum(spread.astype(jnp.float32), axis=0)
    return jnp.concatenate([out_z[None], out_xy], axis=0)[None]


def solution(mesh):
    fine = Mesh(np.array(mesh.devices).reshape(SIZES), AXES)
    return jax.shard_map(
        body,
        mesh=fine,
        in_specs=(
            P(("z", "x"), None, None, None),
            P(("z", "x"), ("y", "c"), None, None),
            P(("z", "x"), ("y", "c"), None, None),
            P(("z", "x"), ("y", "c"), None),
        ),
        out_specs=P(("z", "x"), None, ("y", "c"), None),
        check_vma=False,
    )
```

```python
import functools

import jax
import jax.numpy as jnp
import numpy as np
from jax import lax
from jax.experimental import pallas as pl
from jax.experimental.pallas import tpu as pltpu
from jax.sharding import Mesh, PartitionSpec as P

AXES = ("y", "c", "z", "x")
SIZES = (4, 2, 8, 4)
K = 256
TERMS = 32
ROWS = 32
CHUNKS = (4, 4, 8, 16)
LATER_CHUNKS = (16, 16)

VMEM = pl.BlockSpec(memory_space=pltpu.VMEM)
SMEM = pl.BlockSpec(memory_space=pltpu.SMEM)
HBM = pl.BlockSpec(memory_space=pltpu.HBM)
ANY = pl.BlockSpec(memory_space=pl.ANY)


def gray(n):
    return n ^ (n >> 1)


def ring_slot(distance, core):
    return gray(jnp.where(core == 0, (4 - distance) & 3, distance))


def ring_distance(slot, core):
    return jnp.where(core == 0, (4 - gray(slot)) & 3, gray(slot))


HALF = ROWS // 2
PARTS = 6


def layout(part, b_z, b_x, x, c):
    return ring_slot(b_x ^ x, c) * (32 if part % 2 == 0 else 8) + b_z


def row(part, j):
    return j * (8 if part % 2 == 0 else 32)


def add_products(vectors, first, n, target_ref, psi_ref, left_ref, right_ref, keeps, sends):
    y, c, x = (lax.axis_index(a) for a in ("y", "c", "x"))
    cores = (c, 1 - c)
    rows = [
        pl.multiple_of(((y ^ ring_distance(j, core)) * 2 + core) * ROWS, ROWS) for core in cores for j in range(4)
    ]
    left = jnp.concatenate([left_ref[0, first + t, pl.ds(r, ROWS), :] for t in range(n) for r in rows], axis=0)
    turned = [jnp.dot(left, psi_ref[0, v], preferred_element_type=jnp.float32).astype(jnp.bfloat16) for v in vectors]
    for t in range(n):
        product = lax.dot_general(
            jnp.concatenate([a[t * K:(t + 1) * K] for a in turned], axis=0),
            right_ref[0, first + t],
            (((1,), (1,)), ((), ())),
            preferred_element_type=jnp.float32,
        )
        target = target_ref[0, first + t, 0]
        for i in range(2 * len(vectors)):
            part = 2 * vectors[0] + i
            for other, ref in enumerate((keeps[i], sends[i])):
                base = layout(part, target >> 2, target & 3, x, cores[other])
                for j in range(4):
                    begin = i // 2 * K + (other * 4 + j) * ROWS + i % 2 * HALF
                    at = base + row(part, j)
                    ref[at] = (ref[at].astype(jnp.float32) + product[begin:begin + HALF]).astype(jnp.bfloat16)


def first_kernel(target_ref, psi_hbm, left_hbm, right_hbm, *refs):
    keeps, sends = refs[:2], refs[2:4]
    token_ref, psi_ref, left_ref, right_ref, sems = refs[4:]
    copies = [pltpu.make_async_copy(psi_hbm, psi_ref, sems.at[2, 0])]
    first = 0
    for i, n in enumerate(CHUNKS):
        at = pl.ds(first, n)
        copies.append(pltpu.make_async_copy(left_hbm.at[:, at], left_ref.at[:, at], sems.at[0, i]))
        copies.append(pltpu.make_async_copy(right_hbm.at[:, at], right_ref.at[:, at], sems.at[1, i]))
        first += n
    for copy in copies:
        copy.start()
    for ref in (*keeps, *sends, token_ref):
        ref[...] = jnp.zeros_like(ref)
    copies[0].wait()
    first = 0
    for i, n in enumerate(CHUNKS):
        copies[2 * i + 1].wait()
        copies[2 * i + 2].wait()
        add_products((0,), first, n, target_ref, psi_ref, left_ref, right_ref, keeps, sends)
        first += n


def later_kernel(vectors, after_ref, target_ref, psi_ref, left_ref, right_ref, *refs):
    n = 2 * len(vectors)
    keeps, sends, token_ref = refs[:n], refs[n:2 * n], refs[2 * n]
    for ref in (*keeps, *sends, token_ref):
        ref[...] = jnp.zeros_like(ref)
    first = 0
    for n in LATER_CHUNKS:
        add_products(vectors, first, n, target_ref, psi_ref, left_ref, right_ref, keeps, sends)
        first += n


def blocks(n):
    return jax.ShapeDtypeStruct((n, HALF, K), jnp.bfloat16)


TOKEN = jax.ShapeDtypeStruct((8, 128), jnp.float32)
LIMIT = pltpu.CompilerParams(vmem_limit_bytes=24 * 2**20)
SMALL = pl.CostEstimate(flops=1, bytes_accessed=1, transcendentals=0)


def first_products(target, *arrays):
    arrays = [pltpu.with_memory_space_constraint(a, pltpu.HBM) for a in arrays]
    return pl.pallas_call(
        first_kernel,
        in_specs=[SMEM, HBM, HBM, HBM],
        out_specs=[VMEM] * 8,
        out_shape=[blocks(128)] * 4 + [TOKEN] + [jax.ShapeDtypeStruct(a.shape, a.dtype) for a in arrays],
        scratch_shapes=[pltpu.SemaphoreType.DMA((3, len(CHUNKS)))],
        compiler_params=LIMIT,
        cost_estimate=SMALL,
        name="first_products",
    )(target, *arrays)


def later_products(token, vectors, target, *arrays):
    return pl.pallas_call(
        functools.partial(later_kernel, vectors),
        in_specs=[ANY, SMEM, VMEM, VMEM, VMEM],
        out_specs=[VMEM] * (4 * len(vectors) + 1),
        out_shape=[blocks(128)] * (4 * len(vectors)) + [TOKEN],
        compiler_params=LIMIT,
        cost_estimate=SMALL,
        name="later_products",
    )(token, target, *arrays)


def gather_arrays(sums):
    arrays, places = [], []
    for terms in sums:
        for a, _ in terms:
            if not any(a is b for b in arrays):
                arrays.append(a)
        places.append([(next(k for k, b in enumerate(arrays) if b is a), start) for a, start in terms])
    return arrays, places


def combine_kernel(n, places, *refs):
    ins, out, token_ref = refs[1:-2], refs[-2], refs[-1]
    token_ref[...] = jnp.zeros_like(token_ref)
    for s, terms in enumerate(places):

        @pl.loop(0, n, unroll=4)
        def _(i):
            value = sum(ins[k][start + i].astype(jnp.float32) for k, start in terms)
            out[s * n + i] = value.astype(jnp.bfloat16)


def combine(token, n, sums):
    arrays, places = gather_arrays(sums)
    return pl.pallas_call(
        functools.partial(combine_kernel, n, places),
        in_specs=[ANY] + [VMEM] * len(arrays),
        out_specs=[VMEM] * 2,
        out_shape=[blocks(n * len(sums)), TOKEN],
        compiler_params=LIMIT,
        cost_estimate=SMALL,
        name="combine",
    )(token, *arrays)


def permutation(move):
    pairs = []
    for index in range(256):
        place = [int(v) for v in np.unravel_index(index, SIZES)]
        pairs.append((index, int(np.ravel_multi_index(move(*place), SIZES))))
    return pairs


def distance_of(slot, core):
    return (4 - gray(slot)) & 3 if core == 0 else gray(slot)


def core_swap(a):
    return lax.ppermute(a, AXES, permutation(lambda y, c, z, x: (y, 1 - c, z, x)))


def swap(a, y_slot=0, x_slot=0):
    def move(y, c, z, x):
        return (y ^ distance_of(y_slot, c), c, z, x ^ distance_of(x_slot, c))

    return lax.ppermute(a, AXES, permutation(move))


def last_kernel(places, *refs):
    ins, out = refs[1:-1], refs[-1]

    @pl.loop(0, 8)
    def _(b):
        for part, terms in enumerate(places):
            value = sum(ins[k][start + b].astype(jnp.float32) for k, start in terms)
            out[b, part // 2, part % 2 * HALF:(part % 2 + 1) * HALF] = value.astype(jnp.bfloat16)


def last_sends(token, parts):
    arrays, places = gather_arrays(parts)
    return pl.pallas_call(
        functools.partial(last_kernel, places),
        in_specs=[ANY] + [VMEM] * len(arrays),
        out_specs=VMEM,
        out_shape=jax.ShapeDtypeStruct((8, PARTS // 2, ROWS, K), jnp.bfloat16),
        compiler_params=LIMIT,
        cost_estimate=SMALL,
        name="last_sends",
    )(token, *arrays)


ORDER = [
    (1, (0,)), (1, (1,)), (1, (2,)), (1, (3,)), (1, (4,)), (1, (5,)),
    (2, (0, 2)), (2, (1, 3)), (2, (4,)), (2, (5,)),
    (3, (0, 2)), (3, (1, 3)), (3, (4,)), (3, (5,)),
    (4, (0, 2, 4)), (4, (1, 3, 5)),
]


def body(wavefunction, left_operators, right_operators, target_sector):
    parts = []

    def start(sums):
        n = len(sums) // 2
        parts.extend([(sums[i], 0), (core_swap(sums[n + i]), 0)] for i in range(n))

    def run(token, order):
        for step, members in order:
            n = 128 >> step
            out, token = combine(token, n, [[(a, at + n) for a, at in parts[p]] for p in members])
            along_x = (members[0] % 2 == 0) == (step <= 2)
            got = swap(out, **{"x_slot" if along_x else "y_slot": 2 if step % 2 else 1})
            for i, p in enumerate(members):
                parts[p].append((got, i * n))
        return token

    *sums, token, psi, left, right = first_products(target_sector, wavefunction, left_operators, right_operators)
    start(sums)
    *sums, token = later_products(token, (1, 2), target_sector, psi, left, right)
    start(sums)
    token = run(token, ORDER)
    spread = lax.all_to_all(last_sends(token, parts), "z", 0, 0, tiled=True)
    return jnp.sum(spread.astype(jnp.float32), axis=0)[None]


def solution(mesh):
    fine = Mesh(np.array(mesh.devices).reshape(SIZES), AXES)
    return jax.shard_map(
        body,
        mesh=fine,
        in_specs=(
            P(("z", "x"), None, None, None),
            P(("z", "x"), ("y", "c"), None, None),
            P(("z", "x"), ("y", "c"), None, None),
            P(("z", "x"), ("y", "c"), None),
        ),
        out_specs=P(("z", "x"), None, ("y", "c"), None),
        check_vma=False,
    )
```

```python
import functools

import jax
import jax.numpy as jnp
import numpy as np
from jax import lax
from jax.experimental import pallas as pl
from jax.experimental.pallas import tpu as pltpu
from jax.sharding import Mesh, PartitionSpec as P

AXES = ("y", "c", "z", "x")
SIZES = (4, 2, 8, 4)
K = 256
TERMS = 32
ROWS = 32
CHUNKS = (4, 4, 8, 16)
LATER_CHUNKS = (16, 16)

VMEM = pl.BlockSpec(memory_space=pltpu.VMEM)
SMEM = pl.BlockSpec(memory_space=pltpu.SMEM)
HBM = pl.BlockSpec(memory_space=pltpu.HBM)
ANY = pl.BlockSpec(memory_space=pl.ANY)


def gray(n):
    return n ^ (n >> 1)


def ring_slot(distance, core):
    return gray(jnp.where(core == 0, (4 - distance) & 3, distance))


def ring_distance(slot, core):
    return jnp.where(core == 0, (4 - gray(slot)) & 3, gray(slot))


HALF = ROWS // 2
PARTS = 6


def layout(part, b_z, b_x, x, c):
    return ring_slot(b_x ^ x, c) * (32 if part % 2 == 0 else 8) + b_z


def row(part, j):
    return j * (8 if part % 2 == 0 else 32)


def add_products(vectors, first, n, target_ref, psi_ref, left_ref, right_ref, keeps, sends):
    y, c, x = (lax.axis_index(a) for a in ("y", "c", "x"))
    cores = (c, 1 - c)
    rows = [
        pl.multiple_of(((y ^ ring_distance(j, core)) * 2 + core) * ROWS, ROWS) for core in cores for j in range(4)
    ]
    left = jnp.concatenate([left_ref[0, first + t, pl.ds(r, ROWS), :] for t in range(n) for r in rows], axis=0)
    turned = [jnp.dot(left, psi_ref[0, v], preferred_element_type=jnp.float32).astype(jnp.bfloat16) for v in vectors]
    for t in range(n):
        product = lax.dot_general(
            jnp.concatenate([a[t * K:(t + 1) * K] for a in turned], axis=0),
            right_ref[0, first + t],
            (((1,), (1,)), ((), ())),
            preferred_element_type=jnp.float32,
        )
        target = target_ref[first + t]
        for i in range(2 * len(vectors)):
            part = 2 * vectors[0] + i
            for other, ref in enumerate((keeps[i], sends[i])):
                base = layout(part, target >> 2, target & 3, x, cores[other])
                for j in range(4):
                    begin = i // 2 * K + (other * 4 + j) * ROWS + i % 2 * HALF
                    at = base + row(part, j)
                    ref[at] = (ref[at].astype(jnp.float32) + product[begin:begin + HALF]).astype(jnp.bfloat16)


def first_kernel(target_ref, psi_hbm, left_hbm, right_hbm, *refs):
    keeps, sends = refs[:2], refs[2:4]
    token_ref, psi_ref, left_ref, right_ref, sems = refs[4:]
    copies = [pltpu.make_async_copy(psi_hbm, psi_ref, sems.at[2, 0])]
    first = 0
    for i, n in enumerate(CHUNKS):
        at = pl.ds(first, n)
        copies.append(pltpu.make_async_copy(left_hbm.at[:, at], left_ref.at[:, at], sems.at[0, i]))
        copies.append(pltpu.make_async_copy(right_hbm.at[:, at], right_ref.at[:, at], sems.at[1, i]))
        first += n
    for copy in copies:
        copy.start()
    for ref in (*keeps, *sends, token_ref):
        ref[...] = jnp.zeros_like(ref)
    copies[0].wait()
    first = 0
    for i, n in enumerate(CHUNKS):
        copies[2 * i + 1].wait()
        copies[2 * i + 2].wait()
        add_products((0,), first, n, target_ref, psi_ref, left_ref, right_ref, keeps, sends)
        first += n


def later_kernel(vectors, after_ref, target_ref, psi_ref, left_ref, right_ref, *refs):
    n = 2 * len(vectors)
    keeps, sends, token_ref = refs[:n], refs[n:2 * n], refs[2 * n]
    for ref in (*keeps, *sends, token_ref):
        ref[...] = jnp.zeros_like(ref)
    first = 0
    for n in LATER_CHUNKS:
        add_products(vectors, first, n, target_ref, psi_ref, left_ref, right_ref, keeps, sends)
        first += n


def blocks(n):
    return jax.ShapeDtypeStruct((n, HALF, K), jnp.bfloat16)


TOKEN = jax.ShapeDtypeStruct((8, 128), jnp.float32)
LIMIT = pltpu.CompilerParams(vmem_limit_bytes=24 * 2**20)
LONG = pl.CostEstimate(flops=10**11, bytes_accessed=1, transcendentals=0)
SMALL = pl.CostEstimate(flops=1, bytes_accessed=1, transcendentals=0)


def first_products(target, *arrays):
    arrays = [pltpu.with_memory_space_constraint(a, pltpu.HBM) for a in arrays]
    return pl.pallas_call(
        first_kernel,
        in_specs=[SMEM, HBM, HBM, HBM],
        out_specs=[VMEM] * 8,
        out_shape=[blocks(128)] * 4 + [TOKEN] + [jax.ShapeDtypeStruct(a.shape, a.dtype) for a in arrays],
        scratch_shapes=[pltpu.SemaphoreType.DMA((3, len(CHUNKS)))],
        compiler_params=LIMIT,
        cost_estimate=SMALL,
        name="first_products",
    )(target, *arrays)


def later_products(token, vectors, target, *arrays):
    return pl.pallas_call(
        functools.partial(later_kernel, vectors),
        in_specs=[ANY, SMEM, VMEM, VMEM, VMEM],
        out_specs=[VMEM] * (4 * len(vectors) + 1),
        out_shape=[blocks(128)] * (4 * len(vectors)) + [TOKEN],
        compiler_params=LIMIT,
        cost_estimate=SMALL,
        name="later_products",
    )(token, target, *arrays)


def gather_arrays(sums):
    arrays, places = [], []
    for terms in sums:
        for a, _ in terms:
            if not any(a is b for b in arrays):
                arrays.append(a)
        places.append([(next(k for k, b in enumerate(arrays) if b is a), start) for a, start in terms])
    return arrays, places


def combine_kernel(n, places, *refs):
    ins, out, token_ref = refs[1:-2], refs[-2], refs[-1]
    token_ref[...] = jnp.zeros_like(token_ref)
    for s, terms in enumerate(places):

        @pl.loop(0, n, unroll=4)
        def _(i):
            value = sum(ins[k][start + i].astype(jnp.float32) for k, start in terms)
            out[s * n + i] = value.astype(jnp.bfloat16)


def combine(token, n, sums):
    arrays, places = gather_arrays(sums)
    return pl.pallas_call(
        functools.partial(combine_kernel, n, places),
        in_specs=[ANY] + [VMEM] * len(arrays),
        out_specs=[VMEM] * 2,
        out_shape=[blocks(n * len(sums)), TOKEN],
        compiler_params=LIMIT,
        cost_estimate=SMALL,
        name="combine",
    )(token, *arrays)


def absorb_kernel(after_ref, got_ref, token_ref):
    token_ref[...] = jnp.zeros_like(token_ref)


def absorb(token, got, cost):
    return pl.pallas_call(
        absorb_kernel,
        in_specs=[ANY, ANY],
        out_specs=VMEM,
        out_shape=TOKEN,
        compiler_params=LIMIT,
        cost_estimate=cost,
        name="absorb",
    )(token, got)


def permutation(move):
    pairs = []
    for index in range(256):
        place = [int(v) for v in np.unravel_index(index, SIZES)]
        pairs.append((index, int(np.ravel_multi_index(move(*place), SIZES))))
    return pairs


def distance_of(slot, core):
    return (4 - gray(slot)) & 3 if core == 0 else gray(slot)


def core_swap(a):
    return lax.ppermute(a, AXES, permutation(lambda y, c, z, x: (y, 1 - c, z, x)))


def swap(a, y_slot=0, x_slot=0):
    def move(y, c, z, x):
        return (y ^ distance_of(y_slot, c), c, z, x ^ distance_of(x_slot, c))

    return lax.ppermute(a, AXES, permutation(move))


def last_kernel(places, *refs):
    ins, out = refs[1:-1], refs[-1]

    @pl.loop(0, 8)
    def _(b):
        for part, terms in enumerate(places):
            value = sum(ins[k][start + b].astype(jnp.float32) for k, start in terms)
            out[b, part // 2, part % 2 * HALF:(part % 2 + 1) * HALF] = value.astype(jnp.bfloat16)


def last_sends(token, parts):
    arrays, places = gather_arrays(parts)
    return pl.pallas_call(
        functools.partial(last_kernel, places),
        in_specs=[ANY] + [VMEM] * len(arrays),
        out_specs=VMEM,
        out_shape=jax.ShapeDtypeStruct((8, PARTS // 2, ROWS, K), jnp.bfloat16),
        compiler_params=LIMIT,
        cost_estimate=SMALL,
        name="last_sends",
    )(token, *arrays)


WAIT, LONG_WAIT = 0, -1
EARLY = [(1, (0,)), (1, (1,))]
LATE = [
    (1, (2,)), (1, (3,)), (WAIT, (0,)), (LONG_WAIT, (1,)), (1, (4,)), (1, (5,)),
    (2, (0, 2)), (2, (1, 3)), (2, (4,)), (2, (5,)),
    (3, (0, 2)), (3, (1, 3)), (3, (4,)), (3, (5,)), (WAIT, (0,)), (WAIT, (1,)),
    (4, (0, 2, 4)), (4, (1, 3, 5)), (WAIT, (0,)),
]


def body(wavefunction, left_operators, right_operators, target_sector):
    parts = []

    def start(sums):
        n = len(sums) // 2
        parts.extend([(sums[i], 0), (core_swap(sums[n + i]), 0)] for i in range(n))

    def run(token, order):
        for step, members in order:
            if step in (WAIT, LONG_WAIT):
                token = absorb(token, parts[members[0]][-1][0], LONG if step == LONG_WAIT else SMALL)
                continue
            n = 128 >> step
            out, token = combine(token, n, [[(a, at + n) for a, at in parts[p]] for p in members])
            along_x = (members[0] % 2 == 0) == (step <= 2)
            got = swap(out, **{"x_slot" if along_x else "y_slot": 2 if step % 2 else 1})
            for i, p in enumerate(members):
                parts[p].append((got, i * n))
        return token

    target = target_sector.reshape(TERMS)
    *sums, token, psi, left, right = first_products(target, wavefunction, left_operators, right_operators)
    start(sums)
    *sums, token = later_products(token, (1,), target, psi, left, right)
    start(sums)
    token = run(token, EARLY)
    *sums, token = later_products(token, (2,), target, psi, left, right)
    start(sums)
    token = run(token, LATE)
    spread = lax.all_to_all(last_sends(token, parts), "z", 0, 0, tiled=True)
    return jnp.sum(spread.astype(jnp.float32), axis=0)[None]


def solution(mesh):
    fine = Mesh(np.array(mesh.devices).reshape(SIZES), AXES)
    return jax.shard_map(
        body,
        mesh=fine,
        in_specs=(
            P(("z", "x"), None, None, None),
            P(("z", "x"), ("y", "c"), None, None),
            P(("z", "x"), ("y", "c"), None, None),
            P(("z", "x"), ("y", "c"), None),
        ),
        out_specs=P(("z", "x"), None, ("y", "c"), None),
        check_vma=False,
    )
```

```python
import functools

import jax
import jax.numpy as jnp
import numpy as np
from jax import lax
from jax.experimental import pallas as pl
from jax.experimental.pallas import tpu as pltpu
from jax.sharding import Mesh, PartitionSpec as P

AXES = ("y", "c", "z", "x")
SIZES = (4, 2, 8, 4)
K = 256
TERMS = 32
ROWS = 32
CHUNKS = (4, 12, 8, 8)
LATER_CHUNKS = (16, 16)

VMEM = pl.BlockSpec(memory_space=pltpu.VMEM)
SMEM = pl.BlockSpec(memory_space=pltpu.SMEM)
HBM = pl.BlockSpec(memory_space=pltpu.HBM)
ANY = pl.BlockSpec(memory_space=pl.ANY)


def gray(n):
    return n ^ (n >> 1)


def ring_slot(distance, core):
    return gray(jnp.where(core == 0, (4 - distance) & 3, distance))


def ring_distance(slot, core):
    return jnp.where(core == 0, (4 - gray(slot)) & 3, gray(slot))


HALF = ROWS // 2
PARTS = 6


def layout(part, b_z, b_x, x, c):
    return ring_slot(b_x ^ x, c) * (32 if part % 2 == 0 else 8) + b_z


def row(part, j):
    return j * (8 if part % 2 == 0 else 32)


def add_products(vectors, first, n, target_ref, psi_ref, left_ref, right_ref, keeps, sends):
    y, c, x = (lax.axis_index(a) for a in ("y", "c", "x"))
    cores = (c, 1 - c)
    rows = [
        pl.multiple_of(((y ^ ring_distance(j, core)) * 2 + core) * ROWS, ROWS) for core in cores for j in range(4)
    ]
    left = jnp.concatenate([left_ref[0, first + t, pl.ds(r, ROWS), :] for t in range(n) for r in rows], axis=0)
    turned = [jnp.dot(left, psi_ref[0, v], preferred_element_type=jnp.float32).astype(jnp.bfloat16) for v in vectors]
    for t in range(n):
        product = lax.dot_general(
            jnp.concatenate([a[t * K:(t + 1) * K] for a in turned], axis=0),
            right_ref[0, first + t],
            (((1,), (1,)), ((), ())),
            preferred_element_type=jnp.float32,
        )
        target = target_ref[first + t]
        for i in range(2 * len(vectors)):
            part = 2 * vectors[0] + i
            for other, ref in enumerate((keeps[i], sends[i])):
                base = layout(part, target >> 2, target & 3, x, cores[other])
                for j in range(4):
                    begin = i // 2 * K + (other * 4 + j) * ROWS + i % 2 * HALF
                    at = base + row(part, j)
                    ref[at] = (ref[at].astype(jnp.float32) + product[begin:begin + HALF]).astype(jnp.bfloat16)


def first_kernel(target_ref, psi_hbm, left_hbm, right_hbm, *refs):
    keeps, sends = refs[:2], refs[2:4]
    token_ref, psi_ref, left_ref, right_ref, sems = refs[4:]
    copies = [pltpu.make_async_copy(psi_hbm, psi_ref, sems.at[2, 0])]
    first = 0
    for i, n in enumerate(CHUNKS):
        at = pl.ds(first, n)
        copies.append(pltpu.make_async_copy(left_hbm.at[:, at], left_ref.at[:, at], sems.at[0, i]))
        copies.append(pltpu.make_async_copy(right_hbm.at[:, at], right_ref.at[:, at], sems.at[1, i]))
        first += n
    for copy in copies:
        copy.start()
    for ref in (*keeps, *sends, token_ref):
        ref[...] = jnp.zeros_like(ref)
    copies[0].wait()
    first = 0
    for i, n in enumerate(CHUNKS):
        copies[2 * i + 1].wait()
        copies[2 * i + 2].wait()
        add_products((0,), first, n, target_ref, psi_ref, left_ref, right_ref, keeps, sends)
        first += n


def later_kernel(vectors, after_ref, target_ref, psi_ref, left_ref, right_ref, *refs):
    n = 2 * len(vectors)
    keeps, sends, token_ref = refs[:n], refs[n:2 * n], refs[2 * n]
    for ref in (*keeps, *sends, token_ref):
        ref[...] = jnp.zeros_like(ref)
    first = 0
    for n in LATER_CHUNKS:
        add_products(vectors, first, n, target_ref, psi_ref, left_ref, right_ref, keeps, sends)
        first += n


def blocks(n):
    return jax.ShapeDtypeStruct((n, HALF, K), jnp.bfloat16)


TOKEN = jax.ShapeDtypeStruct((8, 128), jnp.float32)
LIMIT = pltpu.CompilerParams(vmem_limit_bytes=24 * 2**20)
LONG = pl.CostEstimate(flops=10**11, bytes_accessed=1, transcendentals=0)
SMALL = pl.CostEstimate(flops=1, bytes_accessed=1, transcendentals=0)


def first_products(target, *arrays):
    arrays = [pltpu.with_memory_space_constraint(a, pltpu.HBM) for a in arrays]
    return pl.pallas_call(
        first_kernel,
        in_specs=[SMEM, HBM, HBM, HBM],
        out_specs=[VMEM] * 8,
        out_shape=[blocks(128)] * 4 + [TOKEN] + [jax.ShapeDtypeStruct(a.shape, a.dtype) for a in arrays],
        scratch_shapes=[pltpu.SemaphoreType.DMA((3, len(CHUNKS)))],
        compiler_params=LIMIT,
        cost_estimate=SMALL,
        name="first_products",
    )(target, *arrays)


def later_products(token, vectors, target, *arrays):
    return pl.pallas_call(
        functools.partial(later_kernel, vectors),
        in_specs=[ANY, SMEM, VMEM, VMEM, VMEM],
        out_specs=[VMEM] * (4 * len(vectors) + 1),
        out_shape=[blocks(128)] * (4 * len(vectors)) + [TOKEN],
        compiler_params=LIMIT,
        cost_estimate=SMALL,
        name="later_products",
    )(token, target, *arrays)


def gather_arrays(sums):
    arrays, places = [], []
    for terms in sums:
        for a, _ in terms:
            if not any(a is b for b in arrays):
                arrays.append(a)
        places.append([(next(k for k, b in enumerate(arrays) if b is a), start) for a, start in terms])
    return arrays, places


def combine_kernel(n, places, *refs):
    ins, out, token_ref = refs[1:-2], refs[-2], refs[-1]
    token_ref[...] = jnp.zeros_like(token_ref)
    for s, terms in enumerate(places):

        @pl.loop(0, n, unroll=4)
        def _(i):
            value = sum(ins[k][start + i].astype(jnp.float32) for k, start in terms)
            out[s * n + i] = value.astype(jnp.bfloat16)


def combine(token, n, sums):
    arrays, places = gather_arrays(sums)
    return pl.pallas_call(
        functools.partial(combine_kernel, n, places),
        in_specs=[ANY] + [VMEM] * len(arrays),
        out_specs=[VMEM] * 2,
        out_shape=[blocks(n * len(sums)), TOKEN],
        compiler_params=LIMIT,
        cost_estimate=SMALL,
        name="combine",
    )(token, *arrays)


def absorb_kernel(after_ref, got_ref, token_ref):
    token_ref[...] = jnp.zeros_like(token_ref)


def absorb(token, got, cost):
    return pl.pallas_call(
        absorb_kernel,
        in_specs=[ANY, ANY],
        out_specs=VMEM,
        out_shape=TOKEN,
        compiler_params=LIMIT,
        cost_estimate=cost,
        name="absorb",
    )(token, got)


def permutation(move):
    pairs = []
    for index in range(256):
        place = [int(v) for v in np.unravel_index(index, SIZES)]
        pairs.append((index, int(np.ravel_multi_index(move(*place), SIZES))))
    return pairs


def distance_of(slot, core):
    return (4 - gray(slot)) & 3 if core == 0 else gray(slot)


def core_swap(a):
    return lax.ppermute(a, AXES, permutation(lambda y, c, z, x: (y, 1 - c, z, x)))


def swap(a, y_slot=0, x_slot=0):
    def move(y, c, z, x):
        return (y ^ distance_of(y_slot, c), c, z, x ^ distance_of(x_slot, c))

    return lax.ppermute(a, AXES, permutation(move))


def last_kernel(places, *refs):
    ins, out = refs[1:-1], refs[-1]

    @pl.loop(0, 8)
    def _(b):
        for part, terms in enumerate(places):
            value = sum(ins[k][start + b].astype(jnp.float32) for k, start in terms)
            out[b, part // 2, part % 2 * HALF:(part % 2 + 1) * HALF] = value.astype(jnp.bfloat16)


def last_sends(token, parts):
    arrays, places = gather_arrays(parts)
    return pl.pallas_call(
        functools.partial(last_kernel, places),
        in_specs=[ANY] + [VMEM] * len(arrays),
        out_specs=VMEM,
        out_shape=jax.ShapeDtypeStruct((8, PARTS // 2, ROWS, K), jnp.bfloat16),
        compiler_params=LIMIT,
        cost_estimate=SMALL,
        name="last_sends",
    )(token, *arrays)


WAIT, LONG_WAIT = 0, -1
EARLY = [(1, (0,)), (1, (1,))]
LATE = [
    (1, (2,)), (1, (3,)), (WAIT, (0,)), (LONG_WAIT, (1,)), (1, (4,)), (1, (5,)),
    (2, (0, 2)), (2, (1, 3)), (2, (4,)), (2, (5,)),
    (3, (0, 2)), (3, (1, 3)), (3, (4,)), (3, (5,)), (WAIT, (0,)), (WAIT, (1,)),
    (4, (0, 2, 4)), (4, (1, 3, 5)), (WAIT, (0,)),
]


def body(wavefunction, left_operators, right_operators, target_sector):
    parts = []

    def start(sums):
        n = len(sums) // 2
        parts.extend([(sums[i], 0), (core_swap(sums[n + i]), 0)] for i in range(n))

    def run(token, order):
        for step, members in order:
            if step in (WAIT, LONG_WAIT):
                token = absorb(token, parts[members[0]][-1][0], LONG if step == LONG_WAIT else SMALL)
                continue
            n = 128 >> step
            out, token = combine(token, n, [[(a, at + n) for a, at in parts[p]] for p in members])
            along_x = (members[0] % 2 == 0) == (step <= 2)
            got = swap(out, **{"x_slot" if along_x else "y_slot": 2 if step % 2 else 1})
            for i, p in enumerate(members):
                parts[p].append((got, i * n))
        return token

    target = target_sector.reshape(TERMS)
    *sums, token, psi, left, right = first_products(target, wavefunction, left_operators, right_operators)
    start(sums)
    *sums, token = later_products(token, (1,), target, psi, left, right)
    start(sums)
    token = run(token, EARLY)
    *sums, token = later_products(token, (2,), target, psi, left, right)
    start(sums)
    token = run(token, LATE)
    spread = lax.all_to_all(last_sends(token, parts), "z", 0, 0, tiled=True)
    return jnp.sum(spread.astype(jnp.float32), axis=0)[None]


def solution(mesh):
    fine = Mesh(np.array(mesh.devices).reshape(SIZES), AXES)
    return jax.shard_map(
        body,
        mesh=fine,
        in_specs=(
            P(("z", "x"), None, None, None),
            P(("z", "x"), ("y", "c"), None, None),
            P(("z", "x"), ("y", "c"), None, None),
            P(("z", "x"), ("y", "c"), None),
        ),
        out_specs=P(("z", "x"), None, ("y", "c"), None),
        check_vma=False,
    )
```
